32 devices in a mesh: row: 4 (over z), col: 2 (over y), rep: 4 (over x, core).
Axes of the slice: x: 2, y: 2, z: 4, core: 2. Of those that a mesh axis runs over, the one named last changes fastest.
Arguments:
- genotypes: bfloat16 [128, 16384], P(('row', 'col', 'rep')), may hold values from 0 to 2, as said below
Outputs:
- main_tiles: float32 [4, 2, 4096, 4096], P('row', 'col', 'rep')
- half_tiles: float32 [4, 4096, 4096], P('row', 'rep', 'col')
The draws below stay inside these ranges and needn't reach their ends.
Inputs may be any that keep to these rules, and one draw needn't show every extreme that they name: `genotypes`: imputed dosages of the alternate allele, real-valued.
All inputs are finite; a program needn't handle non-finite values.
Results may differ from the reference program's by a relative error of at most 0.008.
Values may be sent and summed in bfloat16 or wider, within the bound.
A program may use at most 128 MiB of HBM per device.

```python
import jax
import jax.numpy as jnp
from jax import lax

VARIANTS = 16384
ROWS_DEV = 4
BLOCKS = 4
BLOCK_W = 4096
SAMPLES = 128
N_ROW = 4
N_COL = 2
N_REP = 4


def draw_genotypes(key, part):
    key_rate = jax.random.fold_in(key, 11)
    key_first = jax.random.fold_in(key, 12)
    key_second = jax.random.fold_in(key, 13)
    rate = jax.random.uniform(key_rate, (1, VARIANTS), jnp.float32, 0.05, 0.6)
    sample_pos = jnp.arange(SAMPLES, dtype=jnp.float32)[:, None]
    trend = (SAMPLES + 2.0 * sample_pos) / (3.0 * SAMPLES)
    first_draw = jax.random.uniform(key_first, (SAMPLES, VARIANTS), jnp.float32, 0.0, 1.0)
    second_draw = jax.random.uniform(key_second, (SAMPLES, VARIANTS), jnp.float32, 0.0, 1.0)
    first_allele = jnp.minimum(1.0, 2.0 * rate * trend * first_draw)
    second_allele = jnp.minimum(1.0, 2.0 * rate * trend * second_draw)
    return (first_allele + second_allele).astype(jnp.bfloat16)


def setup_inputs(seed: int = 0) -> dict:
    arg_keys = jax.random.split(jax.random.key(seed), 2)
    genotypes = draw_genotypes(jax.random.fold_in(arg_keys[1], 71), 0)
    return {"genotypes": genotypes}


def reference(genotypes):
    dosage = genotypes.astype(jnp.float32)
    sample_count = dosage.shape[0]
    sum_dose = lax.optimization_barrier(jnp.sum(dosage, axis=0))
    sum_square = lax.optimization_barrier(jnp.sum(dosage * dosage, axis=0))
    average = sum_dose / sample_count
    spread = sum_square / sample_count - average * average
    scaled = ((dosage - average) * lax.rsqrt(spread + 1e-05)).astype(jnp.bfloat16)
    grouped = scaled.reshape(N_ROW * N_COL, N_REP, ROWS_DEV, VARIANTS)
    tile_width = (N_COL + 1) * BLOCK_W
    replica_list = []
    for replica in range(N_REP):
        replica_rows = grouped[:, replica].reshape(-1, VARIANTS).astype(jnp.float32)
        replica_list.append((replica_rows, jnp.concatenate([replica_rows, replica_rows], axis=1)))

    def one_row(block_index):
        running = jnp.zeros((BLOCK_W, tile_width), jnp.float32)
        begin = (block_index * BLOCK_W).astype(jnp.int32)
        for replica_rows, doubled in replica_list:
            left_cols = lax.dynamic_slice_in_dim(replica_rows, begin, BLOCK_W, 1)
            right_cols = lax.dynamic_slice_in_dim(doubled, begin, tile_width, 1)
            portion = jnp.dot(left_cols.T, right_cols, preferred_element_type=jnp.float32, precision=lax.Precision.HIGHEST) * (1.0 / SAMPLES)
            rounded = lax.optimization_barrier(portion.astype(jnp.bfloat16))
            running = running + rounded.astype(jnp.float32)
        return running.reshape(BLOCK_W, N_COL + 1, BLOCK_W).transpose(1, 0, 2)
    all_tiles = lax.map(one_row, jnp.arange(BLOCKS, dtype=jnp.int32))
    return (all_tiles[:, :N_COL], all_tiles[:, N_COL])
```

```python
import functools

import jax
import jax.numpy as jnp
from jax import lax
from jax.experimental import pallas as pl
from jax.experimental.pallas import tpu as pltpu
from jax.sharding import PartitionSpec as P

MESH = pl.DeviceIdType.MESH
SUB = 4


def gather_kernel(sizes, x_ref, out_ref, stage, zbuf, z_send, z_recv, p_send, p_recv, c_send, c_recv, l_sem):
    rows, cols, reps = sizes
    chips = reps // 2
    r, c, q = lax.axis_index("row"), lax.axis_index("col"), lax.axis_index("rep")
    chip, core = q // 2, q % 2
    per_slab = reps // cols
    six = reps + per_slab
    w = stage.shape[-1]
    unit = SUB * w

    def plane(k):
        return ((r + rows - k) % rows, c, q)

    def peer(j):
        c2 = (c + j // chips) % cols
        chip2 = (chip + j % chips) % chips
        return c2, chip2, (r, c2, chip2 * 2 + core)

    partner = (r, c, chip * 2 + (1 - core))
    barrier = pltpu.get_barrier_semaphore()
    friends = [plane(k) for k in range(1, rows)] + [peer(j)[2] for j in range(1, cols * chips)] + [partner]
    for friend in friends:
        pl.semaphore_signal(barrier, inc=1, device_id=friend, device_id_type=MESH)

    for u in range(rows * reps):
        pieces = [x_ref[:, u * unit + j * w : u * unit + (j + 1) * w].astype(jnp.float32) for j in range(SUB)]
        tile = jnp.concatenate(pieces, axis=0).astype(jnp.bfloat16)
        stage[u] = tile
        if u < reps:
            stage[rows * reps + u] = tile

    def plane_pieces(row):
        far = ((row + rows // 2) % rows) * reps
        return (
            (far, 0, per_slab),
            (row * reps, per_slab, 2 * reps),
            (far + per_slab, per_slab + 2 * reps, per_slab),
        )

    for src, dst, count in plane_pieces(r):
        for u in range(count):
            zbuf[0, dst + u] = stage[src + u]
    pl.semaphore_wait(barrier, len(friends))

    def z_copies(k):
        target = plane(k)
        return [
            pltpu.make_async_remote_copy(
                src_ref=stage.at[pl.ds(src, count)],
                dst_ref=zbuf.at[k, pl.ds(dst, count)],
                send_sem=z_send.at[k, i],
                recv_sem=z_recv.at[k, i],
                device_id=target,
                device_id_type=MESH,
            )
            for i, (src, dst, count) in enumerate(plane_pieces(target[0]))
        ]

    def p_copies(k, j):
        c2, chip2, target = peer(j)
        return [
            pltpu.make_async_remote_copy(
                src_ref=zbuf.at[k, pl.ds(src, count)],
                dst_ref=out_ref.at[0, k, j, pl.ds(dst, count)],
                send_sem=p_send.at[k, j, i],
                recv_sem=p_recv.at[k, j, i],
                device_id=target,
                device_id_type=MESH,
            )
            for i, (src, dst, count) in enumerate(((six * c2, 0, six), (per_slab + 2 * chip2, six, 2)))
        ]

    def l_copies(k):
        return [
            pltpu.make_async_copy(
                zbuf.at[k, pl.ds(src, count)], out_ref.at[0, k, 0, pl.ds(dst, count)], l_sem.at[k, i]
            )
            for i, (src, dst, count) in enumerate(((six * c, 0, six), (per_slab + 2 * chip, six, 2)))
        ]

    def c_copies(k):
        return [
            pltpu.make_async_remote_copy(
                src_ref=out_ref.at[0, k, :, pl.ds(at, count)],
                dst_ref=out_ref.at[1, k, :, pl.ds(at, count)],
                send_sem=c_send.at[k, i],
                recv_sem=c_recv.at[k, i],
                device_id=partner,
                device_id_type=MESH,
            )
            for i, (at, count) in enumerate(((0, six), (six, 2)))
        ]

    def spread(k):
        for j in range(cols * chips - 1, 0, -1):
            wide, narrow = p_copies(k, j)
            wide.start()
            pl.when(peer(j)[0] != 0)(narrow.start)
        for copy in l_copies(k):
            copy.start()

    def share(k):
        for copy in l_copies(k):
            copy.wait()
        for j in range(1, cols * chips):
            wide, narrow = p_copies(k, j)
            wide.wait_recv()
            pl.when(c != 0)(narrow.wait_recv)
        wide, narrow = c_copies(k)
        wide.start()
        pl.when(c != 0)(narrow.start)

    order = [k for i in range(1, rows // 2 + 1) for k in ((i, rows - i) if 2 * i != rows else (i,))]
    for k in order:
        for copy in z_copies(k):
            copy.start()
    spread(0)
    before = 0
    for k in order:
        for copy in z_copies(k):
            copy.wait_recv()
        spread(k)
        share(before)
        before = k
    share(before)
    for k in range(rows):
        if k:
            for copy in z_copies(k):
                copy.wait_send()
        for j in range(1, cols * chips):
            wide, narrow = p_copies(k, j)
            wide.wait_send()
            pl.when(peer(j)[0] != 0)(narrow.wait_send)
        wide, narrow = c_copies(k)
        wide.wait()
        pl.when(c != 0)(narrow.wait)


def tile_kernel(sizes, samples, g_ref, main_ref, half_ref, left, right, main_buf, half_buf, sems):
    rows, cols, reps = sizes
    c, q = lax.axis_index("col"), lax.axis_index("rep")
    per_slab = reps // cols
    six = reps + per_slab
    w = g_ref.shape[-1]
    unit = SUB * w
    pairs = g_ref.shape[0] // 2

    def standardized(index, put):
        low = lax.broadcasted_iota(jnp.int32, (pairs, 8, w), 1) < 4
        for m in range(SUB // 2):
            own = g_ref[:pairs, index, 8 * m : 8 * m + 8, :].astype(jnp.float32)
            other = g_ref[pairs:, index, 8 * m : 8 * m + 8, :].astype(jnp.float32)
            even = jnp.where(low, own, pltpu.roll(other, 4, 1))
            odd = jnp.where(low, pltpu.roll(own, 4, 1), other)
            for j, dosage in ((2 * m, even), (2 * m + 1, odd)):
                dosage = dosage.reshape(8 * pairs, w)
                average = jnp.sum(dosage, axis=0, keepdims=True) / samples
                spread = jnp.sum(dosage * dosage, axis=0, keepdims=True) / samples - average * average
                put(j, (dosage - average) * lax.rsqrt(spread + 1e-05))

    def put_left(j, scaled):
        left[j * w : (j + 1) * w, :] = scaled.T.astype(jnp.bfloat16)

    standardized(jnp.where(c == 0, per_slab + q, six + q % 2), put_left)

    copies = []
    for u in range(six):
        slot = u % 2
        index = per_slab * (1 - c) + u if u < reps else reps * c + (u - reps)

        def put_right(j, scaled):
            right[slot, :, j * w : (j + 1) * w] = scaled.astype(jnp.bfloat16)

        standardized(index, put_right)
        buf, ref, at = (main_buf, main_ref.at[0, 0], u) if u < reps else (half_buf, half_ref.at[0], u - reps)
        here = pl.ds(at * unit, unit)
        step = unit // 2
        for i in range(2):
            band = pl.ds(i * step, step)
            buf[band, here] = jnp.dot(
                left[band, :], right[slot], preferred_element_type=jnp.float32
            ) * (1.0 / samples)
            copy = pltpu.make_async_copy(buf.at[band, here], ref.at[band, here], sems.at[u, i])
            copy.start()
            copies.append(copy)
    for copy in copies:
        copy.wait()


def fast_body(sizes, genotypes):
    rows, cols, reps = sizes
    sample_rows, variants = genotypes.shape
    samples = sample_rows * rows * cols * reps
    unit = variants // (rows * reps)
    w = unit // SUB
    chips = reps // 2
    per_slab = reps // cols
    six = reps + per_slab
    near = cols * chips
    dma = pltpu.SemaphoreType.DMA
    gathered = pl.pallas_call(
        functools.partial(gather_kernel, sizes),
        out_shape=jax.ShapeDtypeStruct((2, rows, near, six + 2, 16, w), jnp.bfloat16),
        in_specs=[pl.BlockSpec(memory_space=pltpu.VMEM)],
        out_specs=pl.BlockSpec(memory_space=pl.ANY),
        scratch_shapes=[
            pltpu.VMEM(((rows + 1) * reps, 16, w), jnp.bfloat16),
            pltpu.VMEM((rows, 2 * six, 16, w), jnp.bfloat16),
            dma((rows, 3)),
            dma((rows, 3)),
            dma((rows, near, 2)),
            dma((rows, near, 2)),
            dma((rows, 2)),
            dma((rows, 2)),
            dma((rows, 2)),
        ],
        compiler_params=pltpu.CompilerParams(collective_id=0, has_side_effects=True),
        name="gather_samples",
    )(genotypes)
    gathered = gathered.reshape(2 * rows * near, six + 2, 16, w)
    height = unit
    wide, narrow = reps * unit, per_slab * unit
    return pl.pallas_call(
        functools.partial(tile_kernel, sizes, samples),
        out_shape=(
            jax.ShapeDtypeStruct((1, 1, height, wide), jnp.float32),
            jax.ShapeDtypeStruct((1, height, narrow), jnp.float32),
        ),
        in_specs=[pl.BlockSpec(memory_space=pltpu.VMEM)],
        out_specs=(pl.BlockSpec(memory_space=pl.ANY), pl.BlockSpec(memory_space=pl.ANY)),
        scratch_shapes=[
            pltpu.VMEM((height, samples), jnp.bfloat16),
            pltpu.VMEM((2, samples, unit), jnp.bfloat16),
            pltpu.VMEM((height, wide), jnp.float32),
            pltpu.VMEM((height, narrow), jnp.float32),
            dma((six, 2)),
        ],
        compiler_params=pltpu.CompilerParams(vmem_limit_bytes=48 * 1024 * 1024),
        name="gram_tiles",
    )(gathered)


def body(genotypes):
    sample_rows, variants = genotypes.shape
    row_count = lax.axis_size("row")
    col_count = lax.axis_size("col")
    rep_count = lax.axis_size("rep")
    sample_count = sample_rows * row_count * col_count * rep_count
    block_width = variants // row_count
    slab_width = block_width // col_count
    pair_count = row_count * col_count
    blocked = genotypes.reshape(sample_rows, row_count, block_width)
    shifted = [jnp.roll(blocked, -bcol, axis=1) for bcol in range(col_count)]
    partner = jnp.stack(shifted, axis=2).reshape(sample_rows, pair_count, block_width)
    slab_view = genotypes.reshape(sample_rows, pair_count, slab_width)
    far_slab = jnp.roll(slab_view, -(pair_count // 2), axis=1)
    own_block = jnp.broadcast_to(
        blocked[:, :, None, :], (sample_rows, row_count, col_count, block_width)
    )
    payload = jnp.concatenate(
        [partner, own_block.reshape(sample_rows, pair_count, block_width), far_slab], axis=2
    )
    payload_width = payload.shape[2]
    arrived = lax.all_to_all(payload, ("row", "col"), split_axis=1, concat_axis=0, tiled=True)
    arrived = arrived.reshape(-1, payload_width)
    values = arrived.astype(jnp.float32)
    col_dose, col_square = lax.psum(
        (jnp.sum(values, axis=0), jnp.sum(values * values, axis=0)), "rep"
    )
    col_mean = col_dose / sample_count
    col_spread = col_square / sample_count - col_mean * col_mean
    arrived = ((values - col_mean) * lax.rsqrt(col_spread + 1e-05)).astype(jnp.bfloat16)
    scale_factor = 1.0 / sample_count
    right_side = jnp.concatenate(
        [arrived[:, :block_width], arrived[:, payload_width - slab_width :]], axis=1
    )
    product = lax.dot_general(
        arrived[:, block_width : 2 * block_width],
        right_side,
        (((0,), (0,)), ((), ())),
        preferred_element_type=jnp.float32,
    )
    partial_value = product * scale_factor
    summed = lax.psum_scatter(
        partial_value.astype(jnp.bfloat16), "rep", scatter_dimension=0, tiled=True
    ).astype(jnp.float32)
    main_tile = summed[:, :block_width].reshape(1, 1, -1, block_width)
    half_tile = summed[:, block_width:].reshape(1, -1, slab_width)
    return (main_tile, half_tile)


def solution(mesh):
    sizes = (mesh.shape["row"], mesh.shape["col"], mesh.shape["rep"])

    def local(genotypes):
        unit = genotypes.shape[1] // (sizes[0] * sizes[2])
        fits = sizes[1] == 2 and sizes[2] % 2 == 0 and sizes[0] % 2 == 0
        if fits and genotypes.shape[0] == 4 and unit % (128 * SUB) == 0:
            return fast_body(sizes, genotypes)
        return body(genotypes)

    placed = (P(("row", "col", "rep"), None),)
    return jax.shard_map(
        local,
        mesh=mesh,
        in_specs=placed,
        out_specs=(P("row", "col", "rep", None), P("row", "rep", "col")),
        check_vma=False,
    )
```

```python
import functools

import jax
import jax.numpy as jnp
from jax import lax
from jax.experimental import pallas as pl
from jax.experimental.pallas import tpu as pltpu
from jax.sharding import PartitionSpec as P

MESH = pl.DeviceIdType.MESH
SUB = 4


def gather_kernel(sizes, x_ref, out_ref, stage, zbuf, z_send, z_recv, p_send, p_recv, c_send, c_recv, l_sem):
    rows, cols, reps = sizes
    chips = reps // 2
    r, c, q = lax.axis_index("row"), lax.axis_index("col"), lax.axis_index("rep")
    chip, core = q // 2, q % 2
    per_slab = reps // cols
    six = reps + per_slab
    w = stage.shape[-1]
    unit = SUB * w

    def plane(k):
        return ((r + rows - k) % rows, c, q)

    def peer(j):
        c2 = (c + j // chips) % cols
        chip2 = (chip + j % chips) % chips
        return c2, chip2, (r, c2, chip2 * 2 + core)

    partner = (r, c, chip * 2 + (1 - core))
    barrier = pltpu.get_barrier_semaphore()
    friends = [plane(k) for k in range(1, rows)] + [peer(j)[2] for j in range(1, cols * chips)] + [partner]
    for friend in friends:
        pl.semaphore_signal(barrier, inc=1, device_id=friend, device_id_type=MESH)

    for u in range(rows * reps):
        pieces = [x_ref[:, u * unit + j * w : u * unit + (j + 1) * w].astype(jnp.float32) for j in range(SUB)]
        tile = jnp.concatenate(pieces, axis=0).astype(jnp.bfloat16)
        stage[u] = tile
        if u < reps:
            stage[rows * reps + u] = tile

    def plane_pieces(row):
        far = ((row + rows // 2) % rows) * reps
        return (
            (far, 0, per_slab),
            (row * reps, per_slab, 2 * reps),
            (far + per_slab, per_slab + 2 * reps, per_slab),
        )

    for src, dst, count in plane_pieces(r):
        for u in range(count):
            zbuf[0, dst + u] = stage[src + u]
    pl.semaphore_wait(barrier, len(friends))

    def z_copies(k):
        target = plane(k)
        return [
            pltpu.make_async_remote_copy(
                src_ref=stage.at[pl.ds(src, count)],
                dst_ref=zbuf.at[k, pl.ds(dst, count)],
                send_sem=z_send.at[k, i],
                recv_sem=z_recv.at[k, i],
                device_id=target,
                device_id_type=MESH,
            )
            for i, (src, dst, count) in enumerate(plane_pieces(target[0]))
        ]

    def p_copies(k, j):
        c2, chip2, target = peer(j)
        return [
            pltpu.make_async_remote_copy(
                src_ref=zbuf.at[k, pl.ds(src, count)],
                dst_ref=out_ref.at[0, k, j, pl.ds(dst, count)],
                send_sem=p_send.at[k, j, i],
                recv_sem=p_recv.at[k, j, i],
                device_id=target,
                device_id_type=MESH,
            )
            for i, (src, dst, count) in enumerate(((six * c2, 0, six), (per_slab + 2 * chip2, six, 2)))
        ]

    def l_copies(k):
        return [
            pltpu.make_async_copy(
                zbuf.at[k, pl.ds(src, count)], out_ref.at[0, k, 0, pl.ds(dst, count)], l_sem.at[k, i]
            )
            for i, (src, dst, count) in enumerate(((six * c, 0, six), (per_slab + 2 * chip, six, 2)))
        ]

    def c_copies(k):
        return [
            pltpu.make_async_remote_copy(
                src_ref=out_ref.at[0, k, :, pl.ds(at, count)],
                dst_ref=out_ref.at[1, k, :, pl.ds(at, count)],
                send_sem=c_send.at[k, i],
                recv_sem=c_recv.at[k, i],
                device_id=partner,
                device_id_type=MESH,
            )
            for i, (at, count) in enumerate(((0, six), (six, 2)))
        ]

    def spread(k):
        for j in range(cols * chips - 1, 0, -1):
            wide, narrow = p_copies(k, j)
            wide.start()
            pl.when(peer(j)[0] != 0)(narrow.start)
        for copy in l_copies(k):
            copy.start()

    def share(k):
        for copy in l_copies(k):
            copy.wait()
        for j in range(1, cols * chips):
            wide, narrow = p_copies(k, j)
            wide.wait_recv()
            pl.when(c != 0)(narrow.wait_recv)
        wide, narrow = c_copies(k)
        wide.start()
        pl.when(c != 0)(narrow.start)

    order = [k for i in range(1, rows // 2 + 1) for k in ((i, rows - i) if 2 * i != rows else (i,))]
    for k in order:
        for copy in z_copies(k):
            copy.start()
    spread(0)
    for k in order:
        for copy in z_copies(k):
            copy.wait_recv()
        spread(k)
    for k in [0] + order:
        share(k)
    for k in range(rows):
        if k:
            for copy in z_copies(k):
                copy.wait_send()
        for j in range(1, cols * chips):
            wide, narrow = p_copies(k, j)
            wide.wait_send()
            pl.when(peer(j)[0] != 0)(narrow.wait_send)
        wide, narrow = c_copies(k)
        wide.wait()
        pl.when(c != 0)(narrow.wait)


def tile_kernel(sizes, samples, g_ref, main_ref, half_ref, left, right, main_buf, half_buf, sems):
    rows, cols, reps = sizes
    c, q = lax.axis_index("col"), lax.axis_index("rep")
    per_slab = reps // cols
    six = reps + per_slab
    w = g_ref.shape[-1]
    unit = SUB * w
    pairs = g_ref.shape[0] // 2

    def standardized(index, put):
        low = lax.broadcasted_iota(jnp.int32, (pairs, 8, w), 1) < 4
        for m in range(SUB // 2):
            own = g_ref[:pairs, index, 8 * m : 8 * m + 8, :].astype(jnp.float32)
            other = g_ref[pairs:, index, 8 * m : 8 * m + 8, :].astype(jnp.float32)
            even = jnp.where(low, own, pltpu.roll(other, 4, 1))
            odd = jnp.where(low, pltpu.roll(own, 4, 1), other)
            for j, dosage in ((2 * m, even), (2 * m + 1, odd)):
                dosage = dosage.reshape(8 * pairs, w)
                average = jnp.sum(dosage, axis=0, keepdims=True) / samples
                spread = jnp.sum(dosage * dosage, axis=0, keepdims=True) / samples - average * average
                put(j, (dosage - average) * lax.rsqrt(spread + 1e-05))

    def put_left(j, scaled):
        left[j * w : (j + 1) * w, :] = scaled.T.astype(jnp.bfloat16)

    standardized(jnp.where(c == 0, per_slab + q, six + q % 2), put_left)

    copies = []
    for u in range(six):
        slot = u % 2
        index = per_slab * (1 - c) + u if u < reps else reps * c + (u - reps)

        def put_right(j, scaled):
            right[slot, :, j * w : (j + 1) * w] = scaled.astype(jnp.bfloat16)

        standardized(index, put_right)
        buf, ref, at = (main_buf, main_ref.at[0, 0], u) if u < reps else (half_buf, half_ref.at[0], u - reps)
        here = pl.ds(at * unit, unit)
        step = unit // 2
        for i in range(2):
            band = pl.ds(i * step, step)
            buf[band, here] = jnp.dot(
                left[band, :], right[slot], preferred_element_type=jnp.float32
            ) * (1.0 / samples)
            copy = pltpu.make_async_copy(buf.at[band, here], ref.at[band, here], sems.at[u, i])
            copy.start()
            copies.append(copy)
    for copy in copies:
        copy.wait()


def fast_body(sizes, genotypes):
    rows, cols, reps = sizes
    sample_rows, variants = genotypes.shape
    samples = sample_rows * rows * cols * reps
    unit = variants // (rows * reps)
    w = unit // SUB
    chips = reps // 2
    per_slab = reps // cols
    six = reps + per_slab
    near = cols * chips
    dma = pltpu.SemaphoreType.DMA
    gathered = pl.pallas_call(
        functools.partial(gather_kernel, sizes),
        out_shape=jax.ShapeDtypeStruct((2, rows, near, six + 2, 16, w), jnp.bfloat16),
        in_specs=[pl.BlockSpec(memory_space=pltpu.VMEM)],
        out_specs=pl.BlockSpec(memory_space=pl.ANY),
        scratch_shapes=[
            pltpu.VMEM(((rows + 1) * reps, 16, w), jnp.bfloat16),
            pltpu.VMEM((rows, 2 * six, 16, w), jnp.bfloat16),
            dma((rows, 3)),
            dma((rows, 3)),
            dma((rows, near, 2)),
            dma((rows, near, 2)),
            dma((rows, 2)),
            dma((rows, 2)),
            dma((rows, 2)),
        ],
        compiler_params=pltpu.CompilerParams(collective_id=0, has_side_effects=True, vmem_limit_bytes=4 * 1024 * 1024),
        name="gather_samples",
    )(genotypes)
    gathered = gathered.reshape(2 * rows * near, six + 2, 16, w)
    height = unit
    wide, narrow = reps * unit, per_slab * unit
    return pl.pallas_call(
        functools.partial(tile_kernel, sizes, samples),
        out_shape=(
            jax.ShapeDtypeStruct((1, 1, height, wide), jnp.float32),
            jax.ShapeDtypeStruct((1, height, narrow), jnp.float32),
        ),
        in_specs=[pl.BlockSpec(memory_space=pltpu.VMEM)],
        out_specs=(pl.BlockSpec(memory_space=pl.ANY), pl.BlockSpec(memory_space=pl.ANY)),
        scratch_shapes=[
            pltpu.VMEM((height, samples), jnp.bfloat16),
            pltpu.VMEM((2, samples, unit), jnp.bfloat16),
            pltpu.VMEM((height, wide), jnp.float32),
            pltpu.VMEM((height, narrow), jnp.float32),
            dma((six, 2)),
        ],
        compiler_params=pltpu.CompilerParams(vmem_limit_bytes=48 * 1024 * 1024),
        name="gram_tiles",
    )(gathered)


def body(genotypes):
    sample_rows, variants = genotypes.shape
    row_count = lax.axis_size("row")
    col_count = lax.axis_size("col")
    rep_count = lax.axis_size("rep")
    sample_count = sample_rows * row_count * col_count * rep_count
    block_width = variants // row_count
    slab_width = block_width // col_count
    pair_count = row_count * col_count
    blocked = genotypes.reshape(sample_rows, row_count, block_width)
    shifted = [jnp.roll(blocked, -bcol, axis=1) for bcol in range(col_count)]
    partner = jnp.stack(shifted, axis=2).reshape(sample_rows, pair_count, block_width)
    slab_view = genotypes.reshape(sample_rows, pair_count, slab_width)
    far_slab = jnp.roll(slab_view, -(pair_count // 2), axis=1)
    own_block = jnp.broadcast_to(
        blocked[:, :, None, :], (sample_rows, row_count, col_count, block_width)
    )
    payload = jnp.concatenate(
        [partner, own_block.reshape(sample_rows, pair_count, block_width), far_slab], axis=2
    )
    payload_width = payload.shape[2]
    arrived = lax.all_to_all(payload, ("row", "col"), split_axis=1, concat_axis=0, tiled=True)
    arrived = arrived.reshape(-1, payload_width)
    values = arrived.astype(jnp.float32)
    col_dose, col_square = lax.psum(
        (jnp.sum(values, axis=0), jnp.sum(values * values, axis=0)), "rep"
    )
    col_mean = col_dose / sample_count
    col_spread = col_square / sample_count - col_mean * col_mean
    arrived = ((values - col_mean) * lax.rsqrt(col_spread + 1e-05)).astype(jnp.bfloat16)
    scale_factor = 1.0 / sample_count
    right_side = jnp.concatenate(
        [arrived[:, :block_width], arrived[:, payload_width - slab_width :]], axis=1
    )
    product = lax.dot_general(
        arrived[:, block_width : 2 * block_width],
        right_side,
        (((0,), (0,)), ((), ())),
        preferred_element_type=jnp.float32,
    )
    partial_value = product * scale_factor
    summed = lax.psum_scatter(
        partial_value.astype(jnp.bfloat16), "rep", scatter_dimension=0, tiled=True
    ).astype(jnp.float32)
    main_tile = summed[:, :block_width].reshape(1, 1, -1, block_width)
    half_tile = summed[:, block_width:].reshape(1, -1, slab_width)
    return (main_tile, half_tile)


def solution(mesh):
    sizes = (mesh.shape["row"], mesh.shape["col"], mesh.shape["rep"])

    def local(genotypes):
        unit = genotypes.shape[1] // (sizes[0] * sizes[2])
        fits = sizes[1] == 2 and sizes[2] % 2 == 0 and sizes[0] % 2 == 0
        if fits and genotypes.shape[0] == 4 and unit % (128 * SUB) == 0:
            return fast_body(sizes, genotypes)
        return body(genotypes)

    placed = (P(("row", "col", "rep"), None),)
    return jax.shard_map(
        local,
        mesh=mesh,
        in_specs=placed,
        out_specs=(P("row", "col", "rep", None), P("row", "rep", "col")),
        check_vma=False,
    )
```

```python
import functools

import jax
import jax.numpy as jnp
from jax import lax
from jax.experimental import pallas as pl
from jax.experimental.pallas import tpu as pltpu
from jax.sharding import PartitionSpec as P

MESH = pl.DeviceIdType.MESH
SUB = 4


def gather_kernel(sizes, x_ref, out_ref, stage, zbuf, z_send, z_recv, p_send, p_recv, c_send, c_recv, l_sem):
    rows, cols, reps = sizes
    chips = reps // 2
    r, c, q = lax.axis_index("row"), lax.axis_index("col"), lax.axis_index("rep")
    chip, core = q // 2, q % 2
    per_slab = reps // cols
    six = reps + per_slab
    w = stage.shape[-1]
    unit = SUB * w

    def plane(k):
        return ((r + rows - k) % rows, c, q)

    def peer(j):
        c2 = (c + j // chips) % cols
        chip2 = (chip + j % chips) % chips
        return c2, chip2, (r, c2, chip2 * 2 + core)

    partner = (r, c, chip * 2 + (1 - core))
    barrier = pltpu.get_barrier_semaphore()
    friends = [plane(k) for k in range(1, rows)] + [peer(j)[2] for j in range(1, cols * chips)] + [partner]
    for friend in friends:
        pl.semaphore_signal(barrier, inc=1, device_id=friend, device_id_type=MESH)

    for u in range(rows * reps):
        pieces = [x_ref[:, u * unit + j * w : u * unit + (j + 1) * w].astype(jnp.float32) for j in range(SUB)]
        tile = jnp.concatenate(pieces, axis=0).astype(jnp.bfloat16)
        stage[u] = tile
        if u < reps:
            stage[rows * reps + u] = tile

    def plane_pieces(row):
        far = ((row + rows // 2) % rows) * reps
        return (
            (far, 0, per_slab),
            (row * reps, per_slab, 2 * reps),
            (far + per_slab, per_slab + 2 * reps, per_slab),
        )

    for src, dst, count in plane_pieces(r):
        for u in range(count):
            zbuf[0, dst + u] = stage[src + u]
    pl.semaphore_wait(barrier, len(friends))

    def z_copies(k):
        target = plane(k)
        return [
            pltpu.make_async_remote_copy(
                src_ref=stage.at[pl.ds(src, count)],
                dst_ref=zbuf.at[k, pl.ds(dst, count)],
                send_sem=z_send.at[k, i],
                recv_sem=z_recv.at[k, i],
                device_id=target,
                device_id_type=MESH,
            )
            for i, (src, dst, count) in enumerate(plane_pieces(target[0]))
        ]

    def p_copies(k, j):
        c2, chip2, target = peer(j)
        return [
            pltpu.make_async_remote_copy(
                src_ref=zbuf.at[k, pl.ds(src, count)],
                dst_ref=out_ref.at[0, k, j, pl.ds(dst, count)],
                send_sem=p_send.at[k, j, i],
                recv_sem=p_recv.at[k, j, i],
                device_id=target,
                device_id_type=MESH,
            )
            for i, (src, dst, count) in enumerate(((six * c2, 0, six), (per_slab + 2 * chip2, six, 2)))
        ]

    def l_copies(k):
        return [
            pltpu.make_async_copy(
                zbuf.at[k, pl.ds(src, count)], out_ref.at[0, k, 0, pl.ds(dst, count)], l_sem.at[k, i]
            )
            for i, (src, dst, count) in enumerate(((six * c, 0, six), (per_slab + 2 * chip, six, 2)))
        ]

    def c_copies(k):
        return [
            pltpu.make_async_remote_copy(
                src_ref=out_ref.at[0, k, :, pl.ds(at, count)],
                dst_ref=out_ref.at[1, k, :, pl.ds(at, count)],
                send_sem=c_send.at[k, i],
                recv_sem=c_recv.at[k, i],
                device_id=partner,
                device_id_type=MESH,
            )
            for i, (at, count) in enumerate(((0, six), (six, 2)))
        ]

    def spread(k):
        for j in range(cols * chips - 1, 0, -1):
            wide, narrow = p_copies(k, j)
            wide.start()
            pl.when(peer(j)[0] != 0)(narrow.start)
        for copy in l_copies(k):
            copy.start()

    def share(k):
        for copy in l_copies(k):
            copy.wait()
        for j in range(1, cols * chips):
            wide, narrow = p_copies(k, j)
            wide.wait_recv()
            pl.when(c != 0)(narrow.wait_recv)
        wide, narrow = c_copies(k)
        wide.start()
        pl.when(c != 0)(narrow.start)

    order = [k for i in range(1, rows // 2 + 1) for k in ((i, rows - i) if 2 * i != rows else (i,))]
    for k in order:
        for copy in z_copies(k):
            copy.start()
    spread(0)
    for k in order:
        for copy in z_copies(k):
            copy.wait_recv()
        spread(k)
    for k in [0] + order:
        share(k)
    for k in range(rows):
        if k:
            for copy in z_copies(k):
                copy.wait_send()
        for j in range(1, cols * chips):
            wide, narrow = p_copies(k, j)
            wide.wait_send()
            pl.when(peer(j)[0] != 0)(narrow.wait_send)
        wide, narrow = c_copies(k)
        wide.wait()
        pl.when(c != 0)(narrow.wait)


def tile_kernel(sizes, samples, g_ref, main_ref, half_ref, left, right, main_buf, half_buf, sems):
    rows, cols, reps = sizes
    c, q = lax.axis_index("col"), lax.axis_index("rep")
    per_slab = reps // cols
    six = reps + per_slab
    w = g_ref.shape[-1]
    unit = SUB * w
    pairs = g_ref.shape[0] // 2

    def standardized(index, put):
        low = lax.broadcasted_iota(jnp.int32, (pairs, 8, w), 1) < 4
        for m in range(SUB // 2):
            own = g_ref[:pairs, index, 8 * m : 8 * m + 8, :].astype(jnp.float32)
            other = g_ref[pairs:, index, 8 * m : 8 * m + 8, :].astype(jnp.float32)
            even = jnp.where(low, own, pltpu.roll(other, 4, 1))
            odd = jnp.where(low, pltpu.roll(own, 4, 1), other)
            for j, dosage in ((2 * m, even), (2 * m + 1, odd)):
                dosage = dosage.reshape(8 * pairs, w)
                average = jnp.sum(dosage, axis=0, keepdims=True) / samples
                spread = jnp.sum(dosage * dosage, axis=0, keepdims=True) / samples - average * average
                put(j, (dosage - average) * lax.rsqrt(spread + 1e-05))

    def put_left(j, scaled):
        left[j * w : (j + 1) * w, :] = scaled.T.astype(jnp.bfloat16)

    standardized(jnp.where(c == 0, per_slab + q, six + q % 2), put_left)

    copies = []
    for u in range(six):
        slot = u % 2
        index = per_slab * (1 - c) + u if u < reps else reps * c + (u - reps)

        def put_right(j, scaled):
            right[slot, :, j * w : (j + 1) * w] = scaled.astype(jnp.bfloat16)

        standardized(index, put_right)
        buf, ref, at = (main_buf, main_ref.at[0, 0], u) if u < reps else (half_buf, half_ref.at[0], u - reps)
        here = pl.ds(at * unit, unit)
        step = unit // 4
        for i in range(4):
            band = pl.ds(i * step, step)
            buf[band, here] = jnp.dot(
                left[band, :], right[slot], preferred_element_type=jnp.float32
            ) * (1.0 / samples)
            copy = pltpu.make_async_copy(buf.at[band, here], ref.at[band, here], sems.at[u, i])
            copy.start()
            copies.append(copy)
    for copy in copies:
        copy.wait()


def fast_body(sizes, genotypes):
    rows, cols, reps = sizes
    sample_rows, variants = genotypes.shape
    samples = sample_rows * rows * cols * reps
    unit = variants // (rows * reps)
    w = unit // SUB
    chips = reps // 2
    per_slab = reps // cols
    six = reps + per_slab
    near = cols * chips
    dma = pltpu.SemaphoreType.DMA
    gathered = pl.pallas_call(
        functools.partial(gather_kernel, sizes),
        out_shape=jax.ShapeDtypeStruct((2, rows, near, six + 2, 16, w), jnp.bfloat16),
        in_specs=[pl.BlockSpec(memory_space=pltpu.VMEM)],
        out_specs=pl.BlockSpec(memory_space=pl.ANY),
        scratch_shapes=[
            pltpu.VMEM(((rows + 1) * reps, 16, w), jnp.bfloat16),
            pltpu.VMEM((rows, 2 * six, 16, w), jnp.bfloat16),
            dma((rows, 3)),
            dma((rows, 3)),
            dma((rows, near, 2)),
            dma((rows, near, 2)),
            dma((rows, 2)),
            dma((rows, 2)),
            dma((rows, 2)),
        ],
        compiler_params=pltpu.CompilerParams(collective_id=0, has_side_effects=True, vmem_limit_bytes=4 * 1024 * 1024),
        name="gather_samples",
    )(genotypes)
    gathered = gathered.reshape(2 * rows * near, six + 2, 16, w)
    height = unit
    wide, narrow = reps * unit, per_slab * unit
    return pl.pallas_call(
        functools.partial(tile_kernel, sizes, samples),
        out_shape=(
            jax.ShapeDtypeStruct((1, 1, height, wide), jnp.float32),
            jax.ShapeDtypeStruct((1, height, narrow), jnp.float32),
        ),
        in_specs=[pl.BlockSpec(memory_space=pltpu.VMEM)],
        out_specs=(pl.BlockSpec(memory_space=pl.ANY), pl.BlockSpec(memory_space=pl.ANY)),
        scratch_shapes=[
            pltpu.VMEM((height, samples), jnp.bfloat16),
            pltpu.VMEM((2, samples, unit), jnp.bfloat16),
            pltpu.VMEM((height, wide), jnp.float32),
            pltpu.VMEM((height, narrow), jnp.float32),
            dma((six, 4)),
        ],
        compiler_params=pltpu.CompilerParams(vmem_limit_bytes=48 * 1024 * 1024),
        name="gram_tiles",
    )(gathered)


def body(genotypes):
    sample_rows, variants = genotypes.shape
    row_count = lax.axis_size("row")
    col_count = lax.axis_size("col")
    rep_count = lax.axis_size("rep")
    sample_count = sample_rows * row_count * col_count * rep_count
    block_width = variants // row_count
    slab_width = block_width // col_count
    pair_count = row_count * col_count
    blocked = genotypes.reshape(sample_rows, row_count, block_width)
    shifted = [jnp.roll(blocked, -bcol, axis=1) for bcol in range(col_count)]
    partner = jnp.stack(shifted, axis=2).reshape(sample_rows, pair_count, block_width)
    slab_view = genotypes.reshape(sample_rows, pair_count, slab_width)
    far_slab = jnp.roll(slab_view, -(pair_count // 2), axis=1)
    own_block = jnp.broadcast_to(
        blocked[:, :, None, :], (sample_rows, row_count, col_count, block_width)
    )
    payload = jnp.concatenate(
        [partner, own_block.reshape(sample_rows, pair_count, block_width), far_slab], axis=2
    )
    payload_width = payload.shape[2]
    arrived = lax.all_to_all(payload, ("row", "col"), split_axis=1, concat_axis=0, tiled=True)
    arrived = arrived.reshape(-1, payload_width)
    values = arrived.astype(jnp.float32)
    col_dose, col_square = lax.psum(
        (jnp.sum(values, axis=0), jnp.sum(values * values, axis=0)), "rep"
    )
    col_mean = col_dose / sample_count
    col_spread = col_square / sample_count - col_mean * col_mean
    arrived = ((values - col_mean) * lax.rsqrt(col_spread + 1e-05)).astype(jnp.bfloat16)
    scale_factor = 1.0 / sample_count
    right_side = jnp.concatenate(
        [arrived[:, :block_width], arrived[:, payload_width - slab_width :]], axis=1
    )
    product = lax.dot_general(
        arrived[:, block_width : 2 * block_width],
        right_side,
        (((0,), (0,)), ((), ())),
        preferred_element_type=jnp.float32,
    )
    partial_value = product * scale_factor
    summed = lax.psum_scatter(
        partial_value.astype(jnp.bfloat16), "rep", scatter_dimension=0, tiled=True
    ).astype(jnp.float32)
    main_tile = summed[:, :block_width].reshape(1, 1, -1, block_width)
    half_tile = summed[:, block_width:].reshape(1, -1, slab_width)
    return (main_tile, half_tile)


def solution(mesh):
    sizes = (mesh.shape["row"], mesh.shape["col"], mesh.shape["rep"])

    def local(genotypes):
        unit = genotypes.shape[1] // (sizes[0] * sizes[2])
        fits = sizes[1] == 2 and sizes[2] % 2 == 0 and sizes[0] % 2 == 0
        if fits and genotypes.shape[0] == 4 and unit % (128 * SUB) == 0:
            return fast_body(sizes, genotypes)
        return body(genotypes)

    placed = (P(("row", "col", "rep"), None),)
    return jax.shard_map(
        local,
        mesh=mesh,
        in_specs=placed,
        out_specs=(P("row", "col", "rep", None), P("row", "rep", "col")),
        check_vma=False,
    )
```
